256 devices in a mesh: cuts: 4 (over x), gx: 8 (over z_lo, core), gy: 8 (over y, z_hi).
Axes of the slice: x: 4, y: 4, z: 8 (z_hi: 2, z_lo: 4; z = z_hi * 4 + z_lo), core: 2. Of those that a mesh axis runs over, the one named last changes fastest.
Arguments:
- slice_starts: float32 [4, 5, 256, 256, 128], P('cuts', None, 'gx', 'gy'), may hold values from -6 to 6
Outputs:
- new_states: float32 [4, 5, 256, 256, 128], P('cuts', None, 'gx', 'gy')
The draws below stay inside these ranges and needn't reach their ends.
All inputs are finite; a program needn't handle non-finite values.
Results may differ from the reference program's by a relative error of at most 0.00011.
Values sent between devices are 32-bit elements; how exact they have to be, the bound alone decides.
A program may use at most 64 MiB of HBM per device.

```python
import jax
import jax.numpy as jnp

NZ = 128
SLICES = 4
NX = 256
NY = 256


def steps_of(rng, dims, pieces, least, high):
    factor_of = 1.0
    for dim, blocks in pieces:
        draws = jax.random.uniform(jax.random.fold_in(jax.random.fold_in(rng, 6), dim), (blocks,), jnp.float32, least / len(pieces), high / len(pieces))
        factor_of = factor_of * jnp.repeat(jnp.exp(draws), dims[dim] // blocks).reshape((-1,) + (1,) * (len(dims) - 1 - dim))
    return factor_of


def centred(rng, shape, scale, bound, split=(), kind=jnp.bfloat16):
    entries = scale * jax.random.normal(rng, shape, jnp.float32)
    if split:
        entries = entries * steps_of(rng, shape, split, -0.22, 0.18)
    return jnp.clip(entries, -bound, bound).astype(kind)


def setup_inputs(seed: int = 0) -> dict:
    streams_of = jax.random.split(jax.random.key(seed), 2)
    return {
        "slice_starts": centred(streams_of[0], (SLICES, 5, NX, NY, NZ), 1.0, 6.0, ((0, 4), (2, 8), (3, 8)), jnp.float32),
    }


TIME_STEP = 0.1
VISCOSITY = 0.2
DIFFUSIVITY = 0.2
BUOYANCY = 1.0
STRATIFICATION = 1.0
COMPRESSION = 1.0


def tendency(padded, spacing):
    centre = padded[:, 1:-1, 1:-1, 1:-1]
    neighbours = [
        (padded[:, 2:, 1:-1, 1:-1], padded[:, :-2, 1:-1, 1:-1]),
        (padded[:, 1:-1, 2:, 1:-1], padded[:, 1:-1, :-2, 1:-1]),
        (padded[:, 1:-1, 1:-1, 2:], padded[:, 1:-1, 1:-1, :-2])]
    gradients = [(higher - lower_side) / (2.0 * spacing) for higher, lower_side in neighbours]
    neighbour_sum = neighbours[0][0] + neighbours[0][1] + neighbours[1][0] + neighbours[1][1] + neighbours[2][0] + neighbours[2][1]
    laplacian = (neighbour_sum - 6.0 * centre) / (spacing * spacing)
    advected = centre[0] * gradients[0] + centre[1] * gradients[1] + centre[2] * gradients[2]
    velocity_terms = [-advected[component] - gradients[component][4] + VISCOSITY * laplacian[component] for component in range(3)]
    velocity_terms[2] = velocity_terms[2] + BUOYANCY * centre[3]
    heat_term = -advected[3] + STRATIFICATION * centre[2] + DIFFUSIVITY * laplacian[3]
    pressure_term = -COMPRESSION * (gradients[0][0] + gradients[1][1] + gradients[2][2])
    return jnp.stack(velocity_terms + [heat_term, pressure_term])


def advance(padded, spacing, step_size):
    return padded[:, 1:-1, 1:-1, 1:-1] + step_size * tendency(padded, spacing)


def vertical_pad(fields):
    return jnp.pad(fields, ((0, 0), (0, 0), (0, 0), (1, 1)))


def full_pad(fields):
    return vertical_pad(jnp.pad(fields, ((0, 0), (1, 1), (1, 1), (0, 0)), mode="wrap"))


def restrict(fields):
    shape = fields.shape
    blocks = fields.reshape(shape[0], shape[1] // 2, 2, shape[2] // 2, 2, shape[3] // 2, 2)
    return jnp.mean(blocks, axis=(2, 4, 6))


def prolong(coarse):
    shape = coarse.shape
    spread = jnp.broadcast_to(coarse[:, :, None, :, None, :, None], (shape[0], shape[1], 2, shape[2], 2, shape[3], 2))
    return spread.reshape(shape[0], shape[1] * 2, shape[2] * 2, shape[3] * 2)


def coarse_step(coarse):
    return advance(full_pad(coarse), 2.0, 2.0 * TIME_STEP)


def reference(slice_starts):
    results = []
    current = restrict(slice_starts[0])
    for slice_pos in range(SLICES):
        start_fields = slice_starts[slice_pos]
        fine_result = advance(full_pad(advance(full_pad(start_fields), 1.0, TIME_STEP)), 1.0, TIME_STEP)
        correction = fine_result - prolong(coarse_step(restrict(start_fields)))
        coarse_next = coarse_step(current)
        results.append(prolong(coarse_next) + correction)
        current = coarse_next + restrict(correction)
    return jnp.stack(results)
```

```python
import jax
import jax.numpy as jnp
from jax import lax
from jax.experimental import pallas as pl
from jax.experimental.pallas import tpu as pltpu
from jax.sharding import PartitionSpec as P

TIME_STEP = 0.1
VISCOSITY = 0.2
MESH = pl.DeviceIdType.MESH
NB = 32
NC = 16
X0 = 8
FIELDS = range(5)


def stencil(C, E, W, N, S, A, B, top, bottom, spacing, step):
    g = step / (2.0 * spacing)
    k = VISCOSITY * step / (spacing * spacing)
    centre = 1.0 - 6.0 * k
    zero = jnp.zeros_like(C[0])
    gu, gv, gw = g * C[0], g * C[1], g * C[2]
    ce, cw = k - gu, k + gu
    cn, cs = k - gv, k + gv
    ca = jnp.where(top, zero, k - gw)
    cb = jnp.where(bottom, zero, k + gw)
    out = []
    for q in range(4):
        out.append(
            (centre * C[q] + ce * E[q] + cw * W[q])
            + (cn * N[q] + cs * S[q])
            + (ca * A[q] + cb * B[q])
        )
    rise_p = jnp.where(top, zero, A[4]) - jnp.where(bottom, zero, B[4])
    rise_w = jnp.where(top, zero, A[2]) - jnp.where(bottom, zero, B[2])
    out[0] = out[0] - g * (E[4] - W[4])
    out[1] = out[1] - g * (N[4] - S[4])
    out[2] = out[2] + (step * C[3] - g * rise_p)
    out[3] = out[3] + step * C[2]
    out.append(C[4] - g * ((E[0] - W[0]) + (N[1] - S[1]) + rise_w))
    return out


def lanes():
    return lax.broadcasted_iota(jnp.int32, (8, 128), 1)


def sublanes():
    return lax.broadcasted_iota(jnp.int32, (8, 128), 0)


def lane_up(v, n=1):
    return pltpu.roll(v, 128 - n, 1)


def lane_down(v, n=1):
    return pltpu.roll(v, n, 1)


def fine_tile(src, dst, ys, yd, rs, rd, top, bottom):
    C = [src[f, ys, pl.ds(rs, 8), :] for f in FIELDS]
    E = [src[f, ys, pl.ds(rs + 1, 8), :] for f in FIELDS]
    W = [src[f, ys, pl.ds(rs - 1, 8), :] for f in FIELDS]
    N = [src[f, ys + 1, pl.ds(rs, 8), :] for f in FIELDS]
    S = [src[f, ys - 1, pl.ds(rs, 8), :] for f in FIELDS]
    A = [lane_up(c) for c in C]
    B = [lane_down(c) for c in C]
    out = stencil(C, E, W, N, S, A, B, top, bottom, 1.0, TIME_STEP)
    for f in FIELDS:
        dst[f, yd, pl.ds(rd, 8), :] = out[f]


def restrict_row(src, y, x0, even):
    out = []
    for f in FIELDS:
        halves = []
        for base in (x0, x0 + 16):
            total = None
            for plane in (y, y + 1):
                for start in (base, base + 1):
                    part = src[f, plane, pl.ds(start, 8, stride=2), :]
                    total = part if total is None else total + part
            halves.append(total)
        low, high = halves
        out.append(0.125 * jnp.where(even, low + lane_up(low), high + lane_down(high)))
    return out


def coarse_row(C, N, S, H, even, sub, top, bottom):
    E, W = [], []
    for f in FIELDS:
        r_w = pltpu.roll(C[f], 1, 0)
        r_e = pltpu.roll(C[f], 7, 0)
        mixed = jnp.where(sub == 0, jnp.where(even, r_w, H[f]), jnp.where(even, H[f], r_e))
        swapped = jnp.where(even, lane_up(mixed), lane_down(mixed))
        W.append(jnp.where(sub == 0, swapped, r_w))
        E.append(jnp.where(sub == 7, swapped, r_e))
    A = [lane_up(c, 2) for c in C]
    B = [lane_down(c, 2) for c in C]
    return stencil(C, E, W, N, S, A, B, top, bottom, 2.0, 2.0 * TIME_STEP)


def kernel(x_ref, o_ref, s0, s1, fine, rs, hs, gr, cin, hin, cout,
           load_sem, out_sem, halo_send, halo_recv, chain_send, chain_recv):
    n = lax.axis_index("cuts")
    gx = lax.axis_index("gx")
    gy = lax.axis_index("gy")

    def at(dn, dx, dy):
        return (lax.rem(n + 4 + dn, 4), lax.rem(gx + 8 + dx, 8), lax.rem(gy + 8 + dy, 8))

    star = [(0, 0), (1, 0), (-1, 0), (0, 1), (0, -1)]
    partners = [(0, dx, dy) for dx in (-1, 0, 1) for dy in (-1, 0, 1) if (dx, dy) != (0, 0)]
    partners += [(dn, dx, dy) for dn in (1, -1) for dx, dy in star]
    barrier = pltpu.get_barrier_semaphore()
    for p in partners:
        pl.semaphore_signal(barrier, inc=1, device_id=at(*p), device_id_type=MESH)

    @pl.loop(0, NB)
    def _(y):
        pltpu.make_async_copy(
            x_ref.at[:, :, y, :], s0.at[:, y + 2, pl.ds(X0, NB), :], load_sem
        ).start()

    pl.semaphore_wait(barrier, len(partners))

    halos = []

    def send(src, dst, where):
        i = len(halos)
        copy = pltpu.make_async_remote_copy(
            src_ref=src, dst_ref=dst, send_sem=halo_send.at[i], recv_sem=halo_recv.at[i],
            device_id=at(*where), device_id_type=MESH,
        )
        copy.start()
        halos.append(copy)

    own = pl.ds(2, NB)
    for step in range(2):
        send(x_ref.at[:, 30 + step, :, :], s0.at[:, own, 6 + step, :], (0, 1, 0))
        send(x_ref.at[:, step, :, :], s0.at[:, own, 40 + step, :], (0, -1, 0))
    for dx, x_from, x_to in ((1, 31, 7), (-1, 0, 40)):
        for dy, y_from, y_to in ((1, 31, 1), (-1, 0, 34)):
            send(x_ref.at[:, x_from, y_from, :], s0.at[:, y_to, x_to, :], (0, dx, dy))
    rows = pl.ds(X0, NB)
    for step in range(2):
        send(x_ref.at[:, :, 30 + step, :], s0.at[:, step, rows, :], (0, 0, 1))
        send(x_ref.at[:, :, step, :], s0.at[:, 34 + step, rows, :], (0, 0, -1))
    gx_halos, gy_halos = halos[:4], halos[4:]

    lane = lanes()
    sub = sublanes()
    even = lane % 2 == 0
    top, bottom = lane == 127, lane == 0
    ctop, cbottom = lane >= 126, lane <= 1

    def first_plane(y, wide):
        starts = (7, 15, 23, 31, 39) if wide else (8, 16, 24, 32)
        for r in starts:
            fine_tile(s0, s1, y + 2, y + 1, r, r, top, bottom)

    def second_plane(y):
        for r in range(0, NB, 8):
            fine_tile(s1, fine, y + 1, y, r + X0, r, top, bottom)

    def put_rs(j):
        out = restrict_row(s0, 2 * j + 2, X0, even)
        for f in FIELDS:
            rs[f, j + 1] = out[f]

    def put_hs(j):
        for f in FIELDS:
            total = None
            for plane in (2 * j + 2, 2 * j + 3):
                west = s0[f, plane, pl.ds(6, 8), :] + s0[f, plane, pl.ds(7, 8), :]
                east = s0[f, plane, pl.ds(33, 8), :] + s0[f, plane, pl.ds(34, 8), :]
                part = jnp.where(sub == 0, west, east)
                total = part if total is None else total + part
            hs[f, j] = 0.125 * (total + jnp.where(even, lane_up(total), lane_down(total)))

    def coarse_of(state, halo, j):
        C = [state[f, j + 1] for f in FIELDS]
        N = [state[f, j + 2] for f in FIELDS]
        S = [state[f, j] for f in FIELDS]
        H = [halo[f, j] for f in FIELDS]
        return coarse_row(C, N, S, H, even, sub, ctop, cbottom)

    def put_gr(j):
        out = coarse_of(rs, hs, j)
        for f in FIELDS:
            gr[f, j] = out[f]

    def put_rf(j):
        out = restrict_row(fine, 2 * j, 0, even)
        for f in FIELDS:
            cout[f, j] = out[f]

    pltpu.make_async_copy(x_ref, s0.at[:, own, rows, :], load_sem).wait()
    for copy in gx_halos:
        copy.wait_recv()

    pl.loop(1, NB - 1)(lambda y: first_plane(y, True))
    pl.loop(2, NB - 2)(second_plane)

    def early_row(j):
        put_rf(j)

    pl.loop(1, NC - 1)(early_row)

    def chain_copies(k, late):
        copies = []
        edge = k + 1
        if late:
            spans = [(0, edge, 3), (NC - edge, edge, 6)]
        else:
            spans = [(edge, NC - 2 * edge, 0)]

        def add(src, dst, where, i):
            copies.append(pltpu.make_async_remote_copy(
                src_ref=src, dst_ref=dst, send_sem=chain_send.at[i], recv_sem=chain_recv.at[i],
                device_id=at(*where), device_id_type=MESH,
            ))

        if late:
            add(cout.at[:, 0], cin.at[:, NC + 1], (1, 0, -1), 9)
            add(cout.at[:, NC - 1], cin.at[:, 0], (1, 0, 1), 10)
        for first, count, i in spans:
            span = pl.ds(first, count)
            add(cout.at[:, span, 7, :], hin.at[:, span, 0, :], (1, 1, 0), i + 1)
            add(cout.at[:, span, 0, :], hin.at[:, span, 7, :], (1, -1, 0), i + 2)
            add(cout.at[:, span], cin.at[:, pl.ds(first + 1, count)], (1, 0, 0), i)
        return copies

    def start_chain(k, late):
        @pl.when(n == k)
        def _():
            for copy in chain_copies(k, late):
                copy.start()

    def wait_chain(k, late):
        @pl.when(n == k + 1)
        def _():
            for copy in chain_copies(k, late):
                copy.wait_recv()

    start_chain(0, False)

    @pl.loop(0, NC)
    def _(j):
        put_rs(j)
        put_hs(j)

    pl.loop(1, NC - 1)(put_gr)

    for copy in gy_halos:
        copy.wait_recv()

    @pl.loop(0, 2)
    def _(side):
        first_plane(side * 33 - 1, False)
        first_plane(side * 31, True)

    @pl.loop(0, 2)
    def _(side):
        second_plane(side * 30)
        second_plane(side * 30 + 1)

    @pl.loop(0, 2)
    def _(side):
        put_rf(side * 15)

    start_chain(0, True)

    @pl.loop(0, 2)
    def _(side):
        put_rs(side * 17 - 1)

    @pl.loop(0, 2)
    def _(side):
        put_gr(side * 15)

    def write_planes(j):
        for y in (2 * j, 2 * j + 1):
            pltpu.make_async_copy(fine.at[:, y], o_ref.at[:, :, y, :], out_sem).start()

    @pl.when(n == 0)
    def _():
        pl.loop(0, NC)(write_planes)

    def chain_row(j):
        out = coarse_of(cin, hin, j)
        for f in FIELDS:
            d = out[f] - gr[f, j]
            cout[f, j] = cout[f, j] + d
            low = jnp.where(even, d, lane_down(d))
            high = jnp.where(even, lane_up(d), d)
            for y in (2 * j, 2 * j + 1):
                for start, part in ((0, low), (1, low), (16, high), (17, high)):
                    span = pl.ds(start, 8, stride=2)
                    fine[f, y, span, :] = fine[f, y, span, :] + part
        write_planes(j)

    for k in range(3):
        wait_chain(k, False)

    @pl.when(n > 0)
    def _():
        pl.loop(n + 1, NC - 1 - n)(chain_row)

    for k in (1, 2):
        start_chain(k, False)

    for k in range(3):
        wait_chain(k, True)

    @pl.when(n > 0)
    def _():
        pl.loop(0, n + 1)(chain_row)
        pl.loop(NC - 1 - n, NC)(chain_row)

    for k in (1, 2):
        start_chain(k, True)

    for copy in halos:
        copy.wait_send()
    for k in range(3):
        @pl.when(n == k)
        def _():
            for late in (False, True):
                for copy in chain_copies(k, late):
                    copy.wait_send()

    pltpu.make_async_copy(fine, o_ref, out_sem).wait()


def body(slice_starts):
    fields = slice_starts[0]
    f32 = jnp.float32
    out = pl.pallas_call(
        kernel,
        out_shape=jax.ShapeDtypeStruct(fields.shape, f32),
        in_specs=[pl.BlockSpec(memory_space=pl.ANY)],
        out_specs=pl.BlockSpec(memory_space=pl.ANY),
        scratch_shapes=[
            pltpu.VMEM((5, 36, 48, 128), f32),
            pltpu.VMEM((5, 34, 48, 128), f32),
            pltpu.VMEM((5, NB, NB, 128), f32),
            pltpu.VMEM((5, NC + 2, 8, 128), f32),
            pltpu.VMEM((5, NC, 8, 128), f32),
            pltpu.VMEM((5, NC, 8, 128), f32),
            pltpu.VMEM((5, NC + 2, 8, 128), f32),
            pltpu.VMEM((5, NC, 8, 128), f32),
            pltpu.VMEM((5, NC, 8, 128), f32),
            pltpu.SemaphoreType.DMA,
            pltpu.SemaphoreType.DMA,
            pltpu.SemaphoreType.DMA((12,)),
            pltpu.SemaphoreType.DMA((12,)),
            pltpu.SemaphoreType.DMA((11,)),
            pltpu.SemaphoreType.DMA((11,)),
        ],
        compiler_params=pltpu.CompilerParams(
            collective_id=0, has_side_effects=True, vmem_limit_bytes=48 * 1024 * 1024
        ),
    )(fields)
    return out[None]


def solution(mesh):
    return jax.shard_map(
        body,
        mesh=mesh,
        in_specs=(P("cuts", None, "gx", "gy", None),),
        out_specs=P("cuts", None, "gx", "gy", None),
        check_vma=False,
    )
```

```python
import jax
import jax.numpy as jnp
from jax import lax
from jax.experimental import pallas as pl
from jax.experimental.pallas import tpu as pltpu
from jax.sharding import PartitionSpec as P

TIME_STEP = 0.1
VISCOSITY = 0.2
MESH = pl.DeviceIdType.MESH
NB = 32
NC = 16
X0 = 8
FIELDS = range(5)


def stencil(C, E, W, N, S, A, B, top, bottom, spacing, step):
    g = step / (2.0 * spacing)
    k = VISCOSITY * step / (spacing * spacing)
    centre = 1.0 - 6.0 * k
    zero = jnp.zeros_like(C[0])
    gu, gv, gw = g * C[0], g * C[1], g * C[2]
    ce, cw = k - gu, k + gu
    cn, cs = k - gv, k + gv
    ca = jnp.where(top, zero, k - gw)
    cb = jnp.where(bottom, zero, k + gw)
    out = []
    for q in range(4):
        out.append(
            (centre * C[q] + ce * E[q] + cw * W[q])
            + (cn * N[q] + cs * S[q])
            + (ca * A[q] + cb * B[q])
        )
    rise_p = jnp.where(top, zero, A[4]) - jnp.where(bottom, zero, B[4])
    rise_w = jnp.where(top, zero, A[2]) - jnp.where(bottom, zero, B[2])
    out[0] = out[0] - g * (E[4] - W[4])
    out[1] = out[1] - g * (N[4] - S[4])
    out[2] = out[2] + (step * C[3] - g * rise_p)
    out[3] = out[3] + step * C[2]
    out.append(C[4] - g * ((E[0] - W[0]) + (N[1] - S[1]) + rise_w))
    return out


def lanes():
    return lax.broadcasted_iota(jnp.int32, (8, 128), 1)


def sublanes():
    return lax.broadcasted_iota(jnp.int32, (8, 128), 0)


def lane_up(v, n=1):
    return pltpu.roll(v, 128 - n, 1)


def lane_down(v, n=1):
    return pltpu.roll(v, n, 1)


def fine_tile(src, dst, ys, yd, rs, rd, top, bottom):
    C = [src[f, ys, pl.ds(rs, 8), :] for f in FIELDS]
    E = [src[f, ys, pl.ds(rs + 1, 8), :] for f in FIELDS]
    W = [src[f, ys, pl.ds(rs - 1, 8), :] for f in FIELDS]
    N = [src[f, ys + 1, pl.ds(rs, 8), :] for f in FIELDS]
    S = [src[f, ys - 1, pl.ds(rs, 8), :] for f in FIELDS]
    A = [lane_up(c) for c in C]
    B = [lane_down(c) for c in C]
    out = stencil(C, E, W, N, S, A, B, top, bottom, 1.0, TIME_STEP)
    for f in FIELDS:
        dst[f, yd, pl.ds(rd, 8), :] = out[f]


def restrict_row(src, y, x0, even):
    out = []
    for f in FIELDS:
        halves = []
        for base in (x0, x0 + 16):
            total = None
            for plane in (y, y + 1):
                for start in (base, base + 1):
                    part = src[f, plane, pl.ds(start, 8, stride=2), :]
                    total = part if total is None else total + part
            halves.append(total)
        low, high = halves
        out.append(0.125 * jnp.where(even, low + lane_up(low), high + lane_down(high)))
    return out


def coarse_row(C, N, S, H, even, sub, top, bottom):
    E, W = [], []
    for f in FIELDS:
        r_w = pltpu.roll(C[f], 1, 0)
        r_e = pltpu.roll(C[f], 7, 0)
        mixed = jnp.where(sub == 0, jnp.where(even, r_w, H[f]), jnp.where(even, H[f], r_e))
        swapped = jnp.where(even, lane_up(mixed), lane_down(mixed))
        W.append(jnp.where(sub == 0, swapped, r_w))
        E.append(jnp.where(sub == 7, swapped, r_e))
    A = [lane_up(c, 2) for c in C]
    B = [lane_down(c, 2) for c in C]
    return stencil(C, E, W, N, S, A, B, top, bottom, 2.0, 2.0 * TIME_STEP)


def kernel(x_ref, o_ref, s0, s1, fine, rs, hs, gr, cin, hin, cout,
           load_sem, halo_send, halo_recv, chain_send, chain_recv):
    n = lax.axis_index("cuts")
    gx = lax.axis_index("gx")
    gy = lax.axis_index("gy")

    def at(dn, dx, dy):
        return (lax.rem(n + 4 + dn, 4), lax.rem(gx + 8 + dx, 8), lax.rem(gy + 8 + dy, 8))

    star = [(0, 0), (1, 0), (-1, 0), (0, 1), (0, -1)]
    partners = [(0, dx, dy) for dx in (-1, 0, 1) for dy in (-1, 0, 1) if (dx, dy) != (0, 0)]
    partners += [(dn, dx, dy) for dn in (1, -1) for dx, dy in star]
    barrier = pltpu.get_barrier_semaphore()
    for p in partners:
        pl.semaphore_signal(barrier, inc=1, device_id=at(*p), device_id_type=MESH)

    @pl.loop(0, NB)
    def _(y):
        pltpu.make_async_copy(
            x_ref.at[:, :, y, :], s0.at[:, y + 2, pl.ds(X0, NB), :], load_sem
        ).start()

    pl.semaphore_wait(barrier, len(partners))

    halos = []

    def send(src, dst, where):
        i = len(halos)
        copy = pltpu.make_async_remote_copy(
            src_ref=src, dst_ref=dst, send_sem=halo_send.at[i], recv_sem=halo_recv.at[i],
            device_id=at(*where), device_id_type=MESH,
        )
        copy.start()
        halos.append(copy)

    own = pl.ds(2, NB)
    for step in range(2):
        send(x_ref.at[:, 30 + step, :, :], s0.at[:, own, 6 + step, :], (0, 1, 0))
        send(x_ref.at[:, step, :, :], s0.at[:, own, 40 + step, :], (0, -1, 0))
    for dx, x_from, x_to in ((1, 31, 7), (-1, 0, 40)):
        for dy, y_from, y_to in ((1, 31, 1), (-1, 0, 34)):
            send(x_ref.at[:, x_from, y_from, :], s0.at[:, y_to, x_to, :], (0, dx, dy))
    rows = pl.ds(X0, NB)
    for step in range(2):
        send(x_ref.at[:, :, 30 + step, :], s0.at[:, step, rows, :], (0, 0, 1))
        send(x_ref.at[:, :, step, :], s0.at[:, 34 + step, rows, :], (0, 0, -1))
    gx_halos, gy_halos = halos[:4], halos[4:]

    lane = lanes()
    sub = sublanes()
    even = lane % 2 == 0
    top, bottom = lane == 127, lane == 0
    ctop, cbottom = lane >= 126, lane <= 1

    def first_plane(y, wide):
        starts = (7, 15, 23, 31, 39) if wide else (8, 16, 24, 32)
        for r in starts:
            fine_tile(s0, s1, y + 2, y + 1, r, r, top, bottom)

    def second_plane(y):
        for r in range(0, NB, 8):
            fine_tile(s1, fine, y + 1, y, r + X0, r, top, bottom)

    def put_rs(j):
        out = restrict_row(s0, 2 * j + 2, X0, even)
        for f in FIELDS:
            rs[f, j + 1] = out[f]

    def put_hs(j):
        for f in FIELDS:
            total = None
            for plane in (2 * j + 2, 2 * j + 3):
                west = s0[f, plane, pl.ds(6, 8), :] + s0[f, plane, pl.ds(7, 8), :]
                east = s0[f, plane, pl.ds(33, 8), :] + s0[f, plane, pl.ds(34, 8), :]
                part = jnp.where(sub == 0, west, east)
                total = part if total is None else total + part
            hs[f, j] = 0.125 * (total + jnp.where(even, lane_up(total), lane_down(total)))

    def coarse_of(state, halo, j):
        C = [state[f, j + 1] for f in FIELDS]
        N = [state[f, j + 2] for f in FIELDS]
        S = [state[f, j] for f in FIELDS]
        H = [halo[f, j] for f in FIELDS]
        return coarse_row(C, N, S, H, even, sub, ctop, cbottom)

    def put_gr(j):
        out = coarse_of(rs, hs, j)
        for f in FIELDS:
            gr[f, j] = out[f]

    def put_rf(j):
        out = restrict_row(fine, 2 * j, 0, even)
        for f in FIELDS:
            cout[f, j] = out[f]

    pltpu.make_async_copy(x_ref, s0.at[:, own, rows, :], load_sem).wait()
    for copy in gx_halos:
        copy.wait_recv()

    pl.loop(1, NB - 1)(lambda y: first_plane(y, True))
    pl.loop(2, NB - 2)(second_plane)

    def early_row(j):
        put_rf(j)

    pl.loop(1, NC - 1)(early_row)

    def chain_copies(k, late):
        copies = []
        edge = k + 1
        if late:
            spans = [(0, edge, 3), (NC - edge, edge, 6)]
        else:
            spans = [(edge, NC - 2 * edge, 0)]

        def add(src, dst, where, i):
            copies.append(pltpu.make_async_remote_copy(
                src_ref=src, dst_ref=dst, send_sem=chain_send.at[i], recv_sem=chain_recv.at[i],
                device_id=at(*where), device_id_type=MESH,
            ))

        if late:
            add(cout.at[:, 0], cin.at[:, NC + 1], (1, 0, -1), 9)
            add(cout.at[:, NC - 1], cin.at[:, 0], (1, 0, 1), 10)
        for first, count, i in spans:
            span = pl.ds(first, count)
            add(cout.at[:, span, 7, :], hin.at[:, span, 0, :], (1, 1, 0), i + 1)
            add(cout.at[:, span, 0, :], hin.at[:, span, 7, :], (1, -1, 0), i + 2)
            add(cout.at[:, span], cin.at[:, pl.ds(first + 1, count)], (1, 0, 0), i)
        return copies

    def start_chain(k, late):
        @pl.when(n == k)
        def _():
            for copy in chain_copies(k, late):
                copy.start()

    def wait_chain(k, late):
        @pl.when(n == k + 1)
        def _():
            for copy in chain_copies(k, late):
                copy.wait_recv()

    start_chain(0, False)

    @pl.loop(0, NC)
    def _(j):
        put_rs(j)
        put_hs(j)

    pl.loop(1, NC - 1)(put_gr)

    for copy in gy_halos:
        copy.wait_recv()

    @pl.loop(0, 2)
    def _(side):
        first_plane(side * 33 - 1, False)
        first_plane(side * 31, True)

    @pl.loop(0, 2)
    def _(side):
        second_plane(side * 30)
        second_plane(side * 30 + 1)

    @pl.loop(0, 2)
    def _(side):
        put_rf(side * 15)

    start_chain(0, True)

    @pl.loop(0, 2)
    def _(side):
        put_rs(side * 17 - 1)

    @pl.loop(0, 2)
    def _(side):
        put_gr(side * 15)

    @pl.when(n == 0)
    def _():
        @pl.loop(0, NB)
        def _(y):
            for f in FIELDS:
                for x in range(0, NB, 8):
                    o_ref[pl.ds(f * NB * NB + x * NB + y, 8, stride=NB), :] = fine[f, y, pl.ds(x, 8), :]

    def chain_row(j):
        out = coarse_of(cin, hin, j)
        for f in FIELDS:
            d = out[f] - gr[f, j]
            gr[f, j] = d
            cout[f, j] = cout[f, j] + d

    def result_row(j):
        for f in FIELDS:
            d = gr[f, j]
            low = jnp.where(even, d, lane_down(d))
            high = jnp.where(even, lane_up(d), d)
            for y in (2 * j, 2 * j + 1):
                for x, part in ((0, low), (1, low), (16, high), (17, high)):
                    total = fine[f, y, pl.ds(x, 8, stride=2), :] + part
                    o_ref[pl.ds(f * NB * NB + x * NB + y, 8, stride=2 * NB), :] = total

    def start_next(late):
        for k in (1, 2):
            start_chain(k, late)

    for k in range(3):
        wait_chain(k, False)

    @pl.when(n > 0)
    def _():
        pl.loop(n + 1, NC - 1 - n)(chain_row)

    start_next(False)

    @pl.when(n > 0)
    def _():
        pl.loop(n + 1, NC - 1 - n)(result_row)

    for k in range(3):
        wait_chain(k, True)

    @pl.when(n > 0)
    def _():
        pl.loop(0, n + 1)(chain_row)
        pl.loop(NC - 1 - n, NC)(chain_row)

    start_next(True)

    @pl.when(n > 0)
    def _():
        pl.loop(0, n + 1)(result_row)
        pl.loop(NC - 1 - n, NC)(result_row)

    for copy in halos:
        copy.wait_send()
    for k in range(3):
        @pl.when(n == k)
        def _():
            for late in (False, True):
                for copy in chain_copies(k, late):
                    copy.wait_send()


def body(slice_starts):
    fields = slice_starts[0]
    f32 = jnp.float32
    out = pl.pallas_call(
        kernel,
        out_shape=pltpu.VMEM((5 * NB * NB, 128), f32),
        in_specs=[pl.BlockSpec(memory_space=pltpu.HBM)],
        out_specs=pl.BlockSpec(memory_space=pltpu.VMEM),
        scratch_shapes=[
            pltpu.VMEM((5, 36, 48, 128), f32),
            pltpu.VMEM((5, 34, 48, 128), f32),
            pltpu.VMEM((5, NB, NB, 128), f32),
            pltpu.VMEM((5, NC + 2, 8, 128), f32),
            pltpu.VMEM((5, NC, 8, 128), f32),
            pltpu.VMEM((5, NC, 8, 128), f32),
            pltpu.VMEM((5, NC + 2, 8, 128), f32),
            pltpu.VMEM((5, NC, 8, 128), f32),
            pltpu.VMEM((5, NC, 8, 128), f32),
            pltpu.SemaphoreType.DMA,
            pltpu.SemaphoreType.DMA((12,)),
            pltpu.SemaphoreType.DMA((12,)),
            pltpu.SemaphoreType.DMA((11,)),
            pltpu.SemaphoreType.DMA((11,)),
        ],
        compiler_params=pltpu.CompilerParams(
            collective_id=0, has_side_effects=True, vmem_limit_bytes=60 * 1024 * 1024
        ),
    )(fields)
    return out.reshape((1,) + fields.shape)


def solution(mesh):
    return jax.shard_map(
        body,
        mesh=mesh,
        in_specs=(P("cuts", None, "gx", "gy", None),),
        out_specs=P("cuts", None, "gx", "gy", None),
        check_vma=False,
    )
```

```python
import jax
import jax.numpy as jnp
from jax import lax
from jax.experimental import pallas as pl
from jax.experimental.pallas import tpu as pltpu
from jax.sharding import PartitionSpec as P

TIME_STEP = 0.1
VISCOSITY = 0.2
MESH = pl.DeviceIdType.MESH
NB = 32
NC = 16
X0 = 8
FIELDS = range(5)
HALO = 3
PARTS = ((1, 8), (9, 6))


def stencil(C, E, W, N, S, A, B, top, bottom, spacing, step):
    g = step / (2.0 * spacing)
    k = VISCOSITY * step / (spacing * spacing)
    centre = 1.0 - 6.0 * k
    zero = jnp.zeros_like(C[0])
    gu, gv, gw = g * C[0], g * C[1], g * C[2]
    ce, cw = k - gu, k + gu
    cn, cs = k - gv, k + gv
    ca = jnp.where(top, zero, k - gw)
    cb = jnp.where(bottom, zero, k + gw)
    out = []
    for q in range(4):
        out.append(
            (centre * C[q] + ce * E[q] + cw * W[q])
            + (cn * N[q] + cs * S[q])
            + (ca * A[q] + cb * B[q])
        )
    rise_p = jnp.where(top, zero, A[4]) - jnp.where(bottom, zero, B[4])
    rise_w = jnp.where(top, zero, A[2]) - jnp.where(bottom, zero, B[2])
    out[0] = out[0] - g * (E[4] - W[4])
    out[1] = out[1] - g * (N[4] - S[4])
    out[2] = out[2] + (step * C[3] - g * rise_p)
    out[3] = out[3] + step * C[2]
    out.append(C[4] - g * ((E[0] - W[0]) + (N[1] - S[1]) + rise_w))
    return out


def lanes():
    return lax.broadcasted_iota(jnp.int32, (8, 128), 1)


def sublanes():
    return lax.broadcasted_iota(jnp.int32, (8, 128), 0)


def lane_up(v, n=1):
    return pltpu.roll(v, 128 - n, v.ndim - 1)


def lane_down(v, n=1):
    return pltpu.roll(v, n, v.ndim - 1)


def fine_tile(src, dst, ys, yd, rs, rd, top, bottom):
    C = [src[f, ys, pl.ds(rs, 8), :] for f in FIELDS]
    E = [src[f, ys, pl.ds(rs + 1, 8), :] for f in FIELDS]
    W = [src[f, ys, pl.ds(rs - 1, 8), :] for f in FIELDS]
    N = [src[f, ys + 1, pl.ds(rs, 8), :] for f in FIELDS]
    S = [src[f, ys - 1, pl.ds(rs, 8), :] for f in FIELDS]
    A = [lane_up(c) for c in C]
    B = [lane_down(c) for c in C]
    out = stencil(C, E, W, N, S, A, B, top, bottom, 1.0, TIME_STEP)
    for f in FIELDS:
        dst[f, yd, pl.ds(rd, 8), :] = out[f]


def restrict_row(src, y, x0, even):
    out = []
    for f in FIELDS:
        halves = []
        for base in (x0, x0 + 16):
            total = None
            for plane in (y, y + 1):
                for start in (base, base + 1):
                    part = src[f, plane, pl.ds(start, 8, stride=2), :]
                    total = part if total is None else total + part
            halves.append(total)
        low, high = halves
        out.append(0.125 * jnp.where(even, low + lane_up(low), high + lane_down(high)))
    return out


def coarse_row(C, N, S, H, even, sub, top, bottom):
    E, W = [], []
    for f in FIELDS:
        r_w = pltpu.roll(C[f], 1, 0)
        r_e = pltpu.roll(C[f], 7, 0)
        mixed = jnp.where(sub == 0, jnp.where(even, r_w, H[f]), jnp.where(even, H[f], r_e))
        swapped = jnp.where(even, lane_up(mixed), lane_down(mixed))
        W.append(jnp.where(sub == 0, swapped, r_w))
        E.append(jnp.where(sub == 7, swapped, r_e))
    A = [lane_up(c, 2) for c in C]
    B = [lane_down(c, 2) for c in C]
    return stencil(C, E, W, N, S, A, B, top, bottom, 2.0, 2.0 * TIME_STEP)


def strip_rows(state, y, count, start, top, bottom):
    rows = pl.ds(y + HALO, count)
    here, east, west = (pl.ds(start + shift, 8) for shift in (0, 1, -1))
    C = [state[f, rows, here, :] for f in FIELDS]
    E = [state[f, rows, east, :] for f in FIELDS]
    W = [state[f, rows, west, :] for f in FIELDS]
    N = [state[f, pl.ds(y + HALO + 1, count), here, :] for f in FIELDS]
    S = [state[f, pl.ds(y + HALO - 1, count), here, :] for f in FIELDS]
    A = [lane_up(c, 2) for c in C]
    B = [lane_down(c, 2) for c in C]
    return stencil(C, E, W, N, S, A, B, top, bottom, 2.0, 2.0 * TIME_STEP)


def kernel(x_ref, o_ref, s0, s1, fine, rs, hs, gr, cout, chain0, chain1, chain2, rim0, rim1, rim2,
           packed0, packed1, packed2, edge0, edge1, edge2, late_own, late_rim, load_sem, halo_send, halo_recv, chain_send, chain_recv, pass_send, pass_recv):
    n = lax.axis_index("cuts")
    gx = lax.axis_index("gx")
    gy = lax.axis_index("gy")
    chain, rim = (chain0, chain1, chain2), (rim0, rim1, rim2)
    packed, edge = (packed0, packed1, packed2), (edge0, edge1, edge2)

    def at(dn, dx, dy):
        return (lax.rem(n + 4 + dn, 4), lax.rem(gx + 8 + dx, 8), lax.rem(gy + 8 + dy, 8))

    def remote(src, dst, where, send_sem, recv_sem):
        return pltpu.make_async_remote_copy(
            src_ref=src, dst_ref=dst, send_sem=send_sem, recv_sem=recv_sem,
            device_id=at(*where), device_id_type=MESH,
        )

    partners = [(0, dx, dy) for dx in (0, 1, -1) for dy in (1, -1, 0) if (dx, dy) != (0, 0)]
    partners += [(dn, 0, dy) for dn in (1, 2, 3) for dy in (1, -1, 0)]
    barrier = pltpu.get_barrier_semaphore()
    for p in partners:
        pl.semaphore_signal(barrier, inc=1, device_id=at(*p), device_id_type=MESH)

    @pl.loop(0, NB)
    def _(y):
        pltpu.make_async_copy(
            x_ref.at[:, :, y, :], s0.at[:, y + 2, pl.ds(X0, NB), :], load_sem
        ).start()

    pl.semaphore_wait(barrier, len(partners))

    halos = []

    def send(src, dst, dx, dy):
        i = len(halos)
        copy = remote(src, dst, (0, dx, dy), halo_send.at[i], halo_recv.at[i])
        copy.start()
        halos.append(copy)

    own, rows = pl.ds(2, NB), pl.ds(X0, NB)
    for step in range(2):
        send(x_ref.at[:, 30 + step, :, :], s0.at[:, own, 6 + step, :], 1, 0)
        send(x_ref.at[:, step, :, :], s0.at[:, own, 40 + step, :], -1, 0)
    for dx, x_from, x_to in ((1, 31, 7), (-1, 0, 40)):
        for dy, y_from, y_to in ((1, 31, 1), (-1, 0, 34)):
            send(x_ref.at[:, x_from, y_from, :], s0.at[:, y_to, x_to, :], dx, dy)

    lane, sub = lanes(), sublanes()
    even = lane % 2 == 0
    top, bottom = lane == 127, lane == 0
    ctop, cbottom = lane >= 126, lane <= 1

    def first_plane(y, starts):
        for r in starts:
            fine_tile(s0, s1, y + 2, y + 1, r, r, top, bottom)

    def second_plane(y, starts):
        for r in starts:
            fine_tile(s1, fine, y + 1, y, r + X0, r, top, bottom)

    def put_rs(j):
        out = restrict_row(s0, 2 * j + 2, X0, even)
        for f in FIELDS:
            rs[f, j + 1] = out[f]

    def put_hs(j):
        for f in FIELDS:
            total = None
            for plane in (2 * j + 2, 2 * j + 3):
                west = s0[f, plane, pl.ds(6, 8), :] + s0[f, plane, pl.ds(7, 8), :]
                east = s0[f, plane, pl.ds(33, 8), :] + s0[f, plane, pl.ds(34, 8), :]
                part = jnp.where(sub == 0, west, east)
                total = part if total is None else total + part
            hs[f, j] = 0.125 * (total + jnp.where(even, lane_up(total), lane_down(total)))

    def put_gr(j):
        C = [rs[f, j + 1] for f in FIELDS]
        N = [rs[f, j + 2] for f in FIELDS]
        S = [rs[f, j] for f in FIELDS]
        H = [hs[f, j] for f in FIELDS]
        out = coarse_row(C, N, S, H, even, sub, ctop, cbottom)
        for f in FIELDS:
            gr[f, j] = out[f]

    def put_e(j):
        out = restrict_row(fine, 2 * j, 0, even)
        for f in FIELDS:
            cout[f, lax.rem(j + 1, NC)] = out[f] - gr[f, j]

    def pairs(low, high, *jobs):
        @pl.loop(low, high, step=2)
        def _(j):
            for job in jobs:
                job(j)
                job(j + 1)

    pltpu.make_async_copy(x_ref, s0.at[:, own, rows, :], load_sem).wait()
    pairs(1, NB - 1, lambda y: first_plane(y, (15, 23, 31)))
    for copy in halos[:4]:
        copy.wait_send()
    for step in range(2):
        send(x_ref.at[:, :, 30 + step, :], s0.at[:, step, rows, :], 0, 1)
        send(x_ref.at[:, :, step, :], s0.at[:, 34 + step, rows, :], 0, -1)
    pairs(2, NB - 2, lambda y: second_plane(y, (8, 16)))

    @pl.when(n == 0)
    def _():
        gr[...] = jnp.zeros_like(gr)

    @pl.when(n > 0)
    def _():
        pairs(0, NC, put_rs)

    for copy in halos[:4]:
        copy.wait_recv()
    cols = pl.ds(8, 8)
    below, above = HALO - 1, HALO + NC

    def own_copies(k, m, part):
        def copy(src, dst, dy, i):
            return remote(src, dst, (m - k, 0, dy), chain_send.at[m - k - 1, i], chain_recv.at[k, i])

        if part == 3:
            return [
                copy(cout.at[:, pl.ds(0, 2)], late_own.at[k], 0, 1),
                copy(cout.at[:, 0], chain[k].at[:, below, cols, :], 1, 2),
                copy(cout.at[:, 1], chain[k].at[:, above, cols, :], -1, 3),
            ]
        if part == 2:
            if (k, m) != (1, 3):
                return []
            return [
                copy(cout.at[:, 15], chain[k].at[:, below - 1, cols, :], 1, 4),
                copy(cout.at[:, 2], chain[k].at[:, above + 1, cols, :], -1, 5),
            ]
        first, count = PARTS[part]
        dst = chain[k].at[:, pl.ds(HALO + first, count), cols, :]
        return [copy(cout.at[:, pl.ds(first + 1, count)], dst, 0, (0, 6)[part])]

    def start_own(part):
        for k in (0, 1, 2):
            if part == 2 and k != 1:
                continue

            @pl.when(n == k)
            def _():
                for m in (3, 2, 1):
                    if m > k:
                        for copy in own_copies(k, m, part):
                            copy.start()

    def pass_copies(k, m, part):
        copies = []
        wide = m - k

        def add(src, dst, dx, dy):
            i = len(copies) + 6 * part
            copies.append(remote(src, dst, (0, dx, dy), pass_send.at[k, i], pass_recv.at[k, i]))

        low, high = pl.ds(0, wide), pl.ds(8 - wide, wide)
        if part == 2:
            both = pl.ds(0, 2)
            if wide > 1:
                few, last = pl.ds(0, wide - 1), pl.ds(9 - wide, wide - 1)
                add(late_own.at[k, :, 0, last, :], rim[k].at[:, 0, last, :], 1, 1)
                add(late_own.at[k, :, 0, few, :], rim[k].at[:, 0, few, :], -1, 1)
                add(late_own.at[k, :, 1, last, :], rim[k].at[:, 1, last, :], 1, -1)
                add(late_own.at[k, :, 1, few, :], rim[k].at[:, 1, few, :], -1, -1)
            add(late_own.at[k, :, both, high, :], late_rim.at[k, :, both, high, :], 1, 0)
            add(late_own.at[k, :, both, low, :], late_rim.at[k, :, both, low, :], -1, 0)
            return copies
        span = (pl.ds(0, 4), pl.ds(4, 3))[part]
        add(packed[k].at[:, span, high, :], edge[k].at[:, span, high, :], 1, 0)
        add(packed[k].at[:, span, low, :], edge[k].at[:, span, low, :], -1, 0)
        if wide > 1 and (k, m) != (1, 3):
            deep = wide - 1
            src, dst, dy = ((HALO + 1, above + 1, -1), (above - 1 - deep, below - deep, 1))[part]
            add(chain[k].at[:, pl.ds(src, deep), cols, :], chain[k].at[:, pl.ds(dst, deep), cols, :], 0, dy)
        if wide > 2:
            src, dst, dy = ((HALO + 1, 3, -1), (above - 2, 2, 1))[part]
            add(chain[k].at[:, src, pl.ds(15, 1), :], rim[k].at[:, dst, pl.ds(7, 1), :], 1, dy)
            add(chain[k].at[:, src, pl.ds(8, 1), :], rim[k].at[:, dst, pl.ds(0, 1), :], -1, dy)
        return copies

    def pack(k, part):
        first, count = PARTS[part]
        half = count // 2
        one = chain[k][:, pl.ds(HALO + first, half), cols, :]
        two = chain[k][:, pl.ds(HALO + first + half, half), cols, :]
        upper = jnp.where(even, lane_up(two), one)
        lower = jnp.where(even, one, lane_down(two))
        packed[k][:, pl.ds(4 * part, half)] = jnp.where(sub < 4, lower, upper)

    def hand_on(m, part):
        for k in range(m):
            own_copies(k, m, part)[0].wait_recv()
            pack(k, part)
            for copy in pass_copies(k, m, part):
                copy.start()

    def outer_part(part):
        first, count = PARTS[part]
        pairs((1, 19)[part], (19, 31)[part], lambda y: first_plane(y, (7, 39)))
        pairs(2 * first, 2 * (first + count), lambda y: second_plane(y, (0, 24)))

        @pl.when(n > 0)
        def _():
            pairs(first, first + count, put_hs)
            pairs(first, first + count, put_gr)

        pairs(first, first + count, put_e)
        start_own(part)

    outer_part(0)
    outer_part(1)

    @pl.when(n > 0)
    def _():
        put_hs(0)
        put_hs(NC - 1)

    for m in (1, 2, 3):
        pl.when(n == m)(lambda: hand_on(m, 0))

    for copy in halos[4:]:
        copy.wait_recv()
    start_own(2)

    @pl.loop(0, 2)
    def _(side):
        first_plane(side * 33 - 1, (8, 16, 24, 32))
        first_plane(side * 31, (7, 15, 23, 31, 39))

    @pl.loop(0, 2)
    def _(side):
        second_plane(side * 30, (0, 8, 16, 24))
        second_plane(side * 30 + 1, (0, 8, 16, 24))

    @pl.when(n > 0)
    def _():
        put_rs(-1)
        put_rs(NC)
        put_gr(0)
        put_gr(NC - 1)

    put_e(0)
    put_e(NC - 1)
    start_own(3)

    @pl.when(n == 0)
    def _():
        @pl.loop(0, NB)
        def _(y):
            for f in FIELDS:
                for x in range(0, NB, 8):
                    o_ref[pl.ds(f * NB * NB + x * NB + y, 8, stride=NB), :] = fine[f, y, pl.ds(x, 8), :]

    def widen(k, rows, own_cols, west, east):
        chain[k][:, rows, pl.ds(0, 8), :] = jnp.where(even, west, lane_down(own_cols))
        chain[k][:, rows, pl.ds(16, 8), :] = jnp.where(even, lane_up(own_cols), east)

    def widen_row(k, row, beside):
        widen(k, row, chain[k][:, row, cols, :], lane_up(beside), lane_down(beside))

    def widen_part(k, part):
        first, count = PARTS[part]
        half = count // 2
        beside = edge[k][:, pl.ds(4 * part, half)]
        one, two = (pl.ds(HALO + first + start, half) for start in (0, half))
        widen(k, one, chain[k][:, one, cols, :], lane_up(beside), lane_down(beside))
        widen(k, two, chain[k][:, two, cols, :], beside, beside)

    def level_rows(k, y, count):
        at_rows = pl.ds(y + HALO, count)
        out = [strip_rows(chain[k - 1], y, count, start, ctop, cbottom) for start in (4, 12)]
        for start, part in zip((4, 12), out):
            for f in FIELDS:
                here = (f, at_rows, pl.ds(start, 8), slice(None))
                chain[k][here] = chain[k][here] + part[f]

    def result_rows(m, y, count):
        out = strip_rows(chain[m - 1], y, count, 8, ctop, cbottom)
        for f in FIELDS:
            d = out[f] - gr[f, pl.ds(y, count)]
            low = jnp.where(even, d, lane_down(d))
            high = jnp.where(even, lane_up(d), d)
            for i in range(count):
                for half in range(2):
                    plane = 2 * (y + i) + half
                    for x, part in ((0, low), (1, low), (16, high), (17, high)):
                        total = fine[f, plane, pl.ds(x, 8, stride=2), :] + part[i]
                        o_ref[pl.ds(f * NB * NB + x * NB + plane, 8, stride=2 * NB), :] = total

    def finish(m):
        passes = [[pass_copies(k, m, part) for part in range(3)] for k in range(m)]
        hand_on(m, 1)
        for k in range(m):
            own_copies(k, m, 3)[0].wait_recv()
            for copy in passes[k][2]:
                copy.start()
        for k in range(m):
            for part in (0, 1):
                for copy in passes[k][part]:
                    copy.wait()
                widen_part(k, part)
            if m - k > 2:
                widen_row(k, HALO - 2, rim[k][:, 2])
                widen_row(k, HALO + NC + 1, rim[k][:, 3])
        for k in range(1, m):
            pl.loop(k + 1, NC - 1 - k, step=2)(lambda y: level_rows(k, y, 2))
        pl.loop(m + 1, NC - 1 - m, step=2)(lambda y: result_rows(m, y, 2))
        for k in range(m):
            for copy in passes[k][2]:
                copy.wait()
            for copy in own_copies(k, m, 2) + own_copies(k, m, 3)[1:]:
                copy.wait_recv()
            for i, row in ((0, HALO + NC - 1), (1, HALO)):
                own_cols = late_own[k, :, i]
                chain[k][:, row, cols, :] = own_cols
                beside = late_rim[k, :, i]
                widen(k, row, own_cols, lane_up(beside), lane_down(beside))
            if m - k > 1:
                widen_row(k, below, rim[k][:, 0])
                widen_row(k, above, rim[k][:, 1])
        for k in range(1, m):
            level_rows(k, k - m, m + 1)
            level_rows(k, NC - 1 - k, m + 1)
        result_rows(m, 0, m + 1)
        result_rows(m, NC - 1 - m, m + 1)

    for m in (1, 2, 3):
        pl.when(n == m)(lambda: finish(m))

    for copy in halos[4:]:
        copy.wait_send()
    for k in (0, 1, 2):
        @pl.when(n == k)
        def _():
            for m in range(k + 1, 4):
                for part in range(4):
                    for copy in own_copies(k, m, part):
                        copy.wait_send()


def body(slice_starts):
    fields = slice_starts[0]
    f32 = jnp.float32
    out = pl.pallas_call(
        kernel,
        out_shape=pltpu.VMEM((5 * NB * NB, 128), f32),
        in_specs=[pl.BlockSpec(memory_space=pltpu.HBM)],
        out_specs=pl.BlockSpec(memory_space=pltpu.VMEM),
        scratch_shapes=[
            pltpu.VMEM((5, 36, 48, 128), f32),
            pltpu.VMEM((5, 34, 48, 128), f32),
            pltpu.VMEM((5, NB, NB, 128), f32),
            pltpu.VMEM((5, NC + 2, 8, 128), f32),
            pltpu.VMEM((5, NC, 8, 128), f32),
            pltpu.VMEM((5, NC, 8, 128), f32),
            pltpu.VMEM((5, NC, 8, 128), f32),
            *[pltpu.VMEM((5, NC + 2 * HALO, 24, 128), f32) for _ in range(3)],
            *[pltpu.VMEM((5, 4, 8, 128), f32) for _ in range(3)],
            *[pltpu.VMEM((5, 7, 8, 128), f32) for _ in range(3)],
            *[pltpu.VMEM((5, 7, 8, 128), f32) for _ in range(3)],
            pltpu.VMEM((3, 5, 2, 8, 128), f32),
            pltpu.VMEM((3, 5, 2, 8, 128), f32),
            pltpu.SemaphoreType.DMA,
            pltpu.SemaphoreType.DMA((12,)),
            pltpu.SemaphoreType.DMA((12,)),
            pltpu.SemaphoreType.DMA((3, 7)),
            pltpu.SemaphoreType.DMA((3, 7)),
            pltpu.SemaphoreType.DMA((3, 18)),
            pltpu.SemaphoreType.DMA((3, 18)),
        ],
        compiler_params=pltpu.CompilerParams(
            collective_id=0, has_side_effects=True, vmem_limit_bytes=60 * 1024 * 1024
        ),
    )(fields)
    return out.reshape((1,) + fields.shape)


def solution(mesh):
    return jax.shard_map(
        body,
        mesh=mesh,
        in_specs=(P("cuts", None, "gx", "gy", None),),
        out_specs=P("cuts", None, "gx", "gy", None),
        check_vma=False,
    )
```

```python
import jax
import jax.numpy as jnp
from jax import lax
from jax.experimental import pallas as pl
from jax.experimental.pallas import tpu as pltpu
from jax.sharding import PartitionSpec as P

TIME_STEP = 0.1
VISCOSITY = 0.2
MESH = pl.DeviceIdType.MESH
NB = 32
NC = 16
X0 = 8
FIELDS = range(5)
HALO = 3
RELAYED = {(1, 3): 2, (0, 2): 3}
PARTS = ((1, 8), (9, 6))


def stencil(C, E, W, N, S, A, B, top, bottom, spacing, step):
    g = step / (2.0 * spacing)
    k = VISCOSITY * step / (spacing * spacing)
    centre = 1.0 - 6.0 * k
    zero = jnp.zeros_like(C[0])
    gu, gv, gw = g * C[0], g * C[1], g * C[2]
    ce, cw = k - gu, k + gu
    cn, cs = k - gv, k + gv
    ca = jnp.where(top, zero, k - gw)
    cb = jnp.where(bottom, zero, k + gw)
    out = []
    for q in range(4):
        out.append(
            (centre * C[q] + ce * E[q] + cw * W[q])
            + (cn * N[q] + cs * S[q])
            + (ca * A[q] + cb * B[q])
        )
    rise_p = jnp.where(top, zero, A[4]) - jnp.where(bottom, zero, B[4])
    rise_w = jnp.where(top, zero, A[2]) - jnp.where(bottom, zero, B[2])
    out[0] = out[0] - g * (E[4] - W[4])
    out[1] = out[1] - g * (N[4] - S[4])
    out[2] = out[2] + (step * C[3] - g * rise_p)
    out[3] = out[3] + step * C[2]
    out.append(C[4] - g * ((E[0] - W[0]) + (N[1] - S[1]) + rise_w))
    return out


def lanes():
    return lax.broadcasted_iota(jnp.int32, (8, 128), 1)


def sublanes():
    return lax.broadcasted_iota(jnp.int32, (8, 128), 0)


def lane_up(v, n=1):
    return pltpu.roll(v, 128 - n, v.ndim - 1)


def lane_down(v, n=1):
    return pltpu.roll(v, n, v.ndim - 1)


def fine_tile(src, dst, ys, yd, rs, rd, top, bottom):
    C = [src[f, ys, pl.ds(rs, 8), :] for f in FIELDS]
    E = [src[f, ys, pl.ds(rs + 1, 8), :] for f in FIELDS]
    W = [src[f, ys, pl.ds(rs - 1, 8), :] for f in FIELDS]
    N = [src[f, ys + 1, pl.ds(rs, 8), :] for f in FIELDS]
    S = [src[f, ys - 1, pl.ds(rs, 8), :] for f in FIELDS]
    A = [lane_up(c) for c in C]
    B = [lane_down(c) for c in C]
    out = stencil(C, E, W, N, S, A, B, top, bottom, 1.0, TIME_STEP)
    for f in FIELDS:
        dst[f, yd, pl.ds(rd, 8), :] = out[f]


def restrict_row(src, y, x0, even):
    out = []
    for f in FIELDS:
        halves = []
        for base in (x0, x0 + 16):
            total = None
            for plane in (y, y + 1):
                for start in (base, base + 1):
                    part = src[f, plane, pl.ds(start, 8, stride=2), :]
                    total = part if total is None else total + part
            halves.append(total)
        low, high = halves
        out.append(0.125 * jnp.where(even, low + lane_up(low), high + lane_down(high)))
    return out


def coarse_row(C, N, S, H, even, sub, top, bottom):
    E, W = [], []
    for f in FIELDS:
        r_w = pltpu.roll(C[f], 1, 0)
        r_e = pltpu.roll(C[f], 7, 0)
        mixed = jnp.where(sub == 0, jnp.where(even, r_w, H[f]), jnp.where(even, H[f], r_e))
        swapped = jnp.where(even, lane_up(mixed), lane_down(mixed))
        W.append(jnp.where(sub == 0, swapped, r_w))
        E.append(jnp.where(sub == 7, swapped, r_e))
    A = [lane_up(c, 2) for c in C]
    B = [lane_down(c, 2) for c in C]
    return stencil(C, E, W, N, S, A, B, top, bottom, 2.0, 2.0 * TIME_STEP)


def strip_rows(state, y, count, start, top, bottom):
    rows = pl.ds(y + HALO, count)
    here, east, west = (pl.ds(start + shift, 8) for shift in (0, 1, -1))
    C = [state[f, rows, here, :] for f in FIELDS]
    E = [state[f, rows, east, :] for f in FIELDS]
    W = [state[f, rows, west, :] for f in FIELDS]
    N = [state[f, pl.ds(y + HALO + 1, count), here, :] for f in FIELDS]
    S = [state[f, pl.ds(y + HALO - 1, count), here, :] for f in FIELDS]
    A = [lane_up(c, 2) for c in C]
    B = [lane_down(c, 2) for c in C]
    return stencil(C, E, W, N, S, A, B, top, bottom, 2.0, 2.0 * TIME_STEP)


def kernel(x_ref, o_ref, s0, s1, fine, rs, hs, gr, cout, chain0, chain1, chain2, rim0, rim1, rim2,
           packed0, packed1, packed2, edge0, edge1, edge2, late_own, late_rim, load_sem, halo_send, halo_recv, chain_send, chain_recv, pass_send, pass_recv, ready):
    n = lax.axis_index("cuts")
    gx = lax.axis_index("gx")
    gy = lax.axis_index("gy")
    chain, rim = (chain0, chain1, chain2), (rim0, rim1, rim2)
    packed, edge = (packed0, packed1, packed2), (edge0, edge1, edge2)

    def at(dn, dx, dy):
        return (lax.rem(n + 4 + dn, 4), lax.rem(gx + 8 + dx, 8), lax.rem(gy + 8 + dy, 8))

    def remote(src, dst, where, send_sem, recv_sem):
        return pltpu.make_async_remote_copy(
            src_ref=src, dst_ref=dst, send_sem=send_sem, recv_sem=recv_sem,
            device_id=at(*where), device_id_type=MESH,
        )

    partners = [(0, dx, dy) for dx in (0, 1, -1) for dy in (1, -1, 0) if (dx, dy) != (0, 0)]
    partners += [(dn, 0, 0) for dn in (1, 2, 3)]
    barrier = pltpu.get_barrier_semaphore()
    for p in partners:
        pl.semaphore_signal(barrier, inc=1, device_id=at(*p), device_id_type=MESH)

    @pl.loop(0, NB)
    def _(y):
        pltpu.make_async_copy(
            x_ref.at[:, :, y, :], s0.at[:, y + 2, pl.ds(X0, NB), :], load_sem
        ).start()

    pl.semaphore_wait(barrier, len(partners))
    for dn in (1, 2, 3):
        pl.semaphore_signal(ready, inc=1, device_id=at(dn, 0, 0), device_id_type=MESH)

    halos = []

    def send(src, dst, dx, dy):
        i = len(halos)
        copy = remote(src, dst, (0, dx, dy), halo_send.at[i], halo_recv.at[i])
        copy.start()
        halos.append(copy)

    own, rows = pl.ds(2, NB), pl.ds(X0, NB)
    for step in range(2):
        send(x_ref.at[:, 30 + step, :, :], s0.at[:, own, 6 + step, :], 1, 0)
        send(x_ref.at[:, step, :, :], s0.at[:, own, 40 + step, :], -1, 0)
    for dx, x_from, x_to in ((1, 31, 7), (-1, 0, 40)):
        for dy, y_from, y_to in ((1, 31, 1), (-1, 0, 34)):
            send(x_ref.at[:, x_from, y_from, :], s0.at[:, y_to, x_to, :], dx, dy)

    for step in range(2):
        send(x_ref.at[:, :, 30 + step, :], s0.at[:, step, rows, :], 0, 1)
        send(x_ref.at[:, :, step, :], s0.at[:, 34 + step, rows, :], 0, -1)

    lane, sub = lanes(), sublanes()
    even = lane % 2 == 0
    top, bottom = lane == 127, lane == 0
    ctop, cbottom = lane >= 126, lane <= 1

    def first_plane(y, starts):
        for r in starts:
            fine_tile(s0, s1, y + 2, y + 1, r, r, top, bottom)

    def second_plane(y, starts):
        for r in starts:
            fine_tile(s1, fine, y + 1, y, r + X0, r, top, bottom)

    def put_rs(j):
        out = restrict_row(s0, 2 * j + 2, X0, even)
        for f in FIELDS:
            rs[f, j + 1] = out[f]

    def put_hs(j):
        for f in FIELDS:
            total = None
            for plane in (2 * j + 2, 2 * j + 3):
                west = s0[f, plane, pl.ds(6, 8), :] + s0[f, plane, pl.ds(7, 8), :]
                east = s0[f, plane, pl.ds(33, 8), :] + s0[f, plane, pl.ds(34, 8), :]
                part = jnp.where(sub == 0, west, east)
                total = part if total is None else total + part
            hs[f, j] = 0.125 * (total + jnp.where(even, lane_up(total), lane_down(total)))

    def put_gr(j):
        C = [rs[f, j + 1] for f in FIELDS]
        N = [rs[f, j + 2] for f in FIELDS]
        S = [rs[f, j] for f in FIELDS]
        H = [hs[f, j] for f in FIELDS]
        out = coarse_row(C, N, S, H, even, sub, ctop, cbottom)
        for f in FIELDS:
            gr[f, j] = out[f]

    def put_e(j):
        out = restrict_row(fine, 2 * j, 0, even)
        for f in FIELDS:
            cout[f, lax.rem(j + 1, NC)] = out[f] - gr[f, j]

    def pairs(low, high, *jobs):
        @pl.loop(low, high, step=2)
        def _(j):
            for job in jobs:
                job(j)
                job(j + 1)

    pltpu.make_async_copy(x_ref, s0.at[:, own, rows, :], load_sem).wait()
    pairs(1, NB - 1, lambda y: first_plane(y, (15, 23, 31)))
    pairs(2, NB - 2, lambda y: second_plane(y, (8, 16)))

    @pl.when(n == 0)
    def _():
        gr[...] = jnp.zeros_like(gr)

    @pl.when(n > 0)
    def _():
        pairs(0, NC, put_rs)

    for copy in halos[:4]:
        copy.wait_recv()
    cols = pl.ds(8, 8)
    below, above = HALO - 1, HALO + NC

    def own_copies(k, m, part):
        def copy(src, dst, dy, i):
            return remote(src, dst, (m - k, 0, dy), chain_send.at[m - k - 1, i], chain_recv.at[k, i])

        if part == 3:
            copies = [
                copy(cout.at[:, pl.ds(0, 2)], late_own.at[k], 0, 1),
                copy(cout.at[:, 0], chain[k].at[:, below, cols, :], 1, 2),
                copy(cout.at[:, 1], chain[k].at[:, above, cols, :], -1, 3),
            ]
            few = m - k - 1
            if few:
                for row, dy in ((0, 1), (1, -1)):
                    for span, dx in ((pl.ds(8 - few, few), 1), (pl.ds(0, few), -1)):
                        i = len(copies) + 4
                        copies.append(remote(
                            cout.at[:, row, span, :], rim[k].at[:, row, span, :], (m - k, dx, dy),
                            chain_send.at[m - k - 1, i], chain_recv.at[k, i],
                        ))
            return copies
        if part == 2:
            if (k, m) != (1, 3):
                return []
            return [
                copy(cout.at[:, 15], chain[k].at[:, below - 1, cols, :], 1, 4),
                copy(cout.at[:, 2], chain[k].at[:, above + 1, cols, :], -1, 5),
            ]
        first, count = PARTS[part]
        dst = chain[k].at[:, pl.ds(HALO + first, count), cols, :]
        i = (0, 6)[part]
        if (k, m) in RELAYED:
            dn = m - RELAYED[k, m]
            return [remote(dst, dst, (dn, 0, 0), chain_send.at[m - k - 1, i], chain_recv.at[k, i])]
        return [copy(cout.at[:, pl.ds(first + 1, count)], dst, 0, i)]

    def start_own(part):
        for k in (0, 1, 2):
            if part == 2 and k != 1:
                continue

            @pl.when(n == k)
            def _():
                for m in (3, 2, 1):
                    if m > k and not (part < 2 and (k, m) in RELAYED):
                        for copy in own_copies(k, m, part):
                            copy.start()

    def pass_copies(k, m, part):
        copies = []
        wide = m - k

        def add(src, dst, dx, dy):
            i = len(copies) + 6 * part
            copies.append(remote(src, dst, (0, dx, dy), pass_send.at[k, i], pass_recv.at[k, i]))

        low, high = pl.ds(0, wide), pl.ds(8 - wide, wide)
        if part == 2:
            both = pl.ds(0, 2)
            add(late_own.at[k, :, both, high, :], late_rim.at[k, :, both, high, :], 1, 0)
            add(late_own.at[k, :, both, low, :], late_rim.at[k, :, both, low, :], -1, 0)
            return copies
        span = (pl.ds(0, 4), pl.ds(4, 3))[part]
        add(packed[k].at[:, span, high, :], edge[k].at[:, span, high, :], 1, 0)
        add(packed[k].at[:, span, low, :], edge[k].at[:, span, low, :], -1, 0)
        if wide > 1 and (k, m) != (1, 3):
            deep = wide - 1
            src, dst, dy = ((HALO + 1, above + 1, -1), (above - 1 - deep, below - deep, 1))[part]
            add(chain[k].at[:, pl.ds(src, deep), cols, :], chain[k].at[:, pl.ds(dst, deep), cols, :], 0, dy)
        if wide > 2:
            src, dst, dy = ((HALO + 1, 3, -1), (above - 2, 2, 1))[part]
            add(chain[k].at[:, src, pl.ds(15, 1), :], rim[k].at[:, dst, pl.ds(7, 1), :], 1, dy)
            add(chain[k].at[:, src, pl.ds(8, 1), :], rim[k].at[:, dst, pl.ds(0, 1), :], -1, dy)
        return copies

    def pack(k, part):
        first, count = PARTS[part]
        half = count // 2
        one = chain[k][:, pl.ds(HALO + first, half), cols, :]
        two = chain[k][:, pl.ds(HALO + first + half, half), cols, :]
        upper = jnp.where(even, lane_up(two), one)
        lower = jnp.where(even, one, lane_down(two))
        packed[k][:, pl.ds(4 * part, half)] = jnp.where(sub < 4, lower, upper)

    def hand_on(m, part):
        for k in ((), (0,), (1, 0), (0, 2, 1))[m]:
            own_copies(k, m, part)[0].wait_recv()
            for (first, last), via in RELAYED.items():
                if (first, via) == (k, m):
                    own_copies(first, last, part)[0].start()
            pack(k, part)
            for copy in pass_copies(k, m, part):
                copy.start()

    def outer_part(part):
        first, count = PARTS[part]
        pairs((1, 19)[part], (19, 31)[part], lambda y: first_plane(y, (7, 39)))
        pairs(2 * first, 2 * (first + count), lambda y: second_plane(y, (0, 24)))

        @pl.when(n > 0)
        def _():
            pairs(first, first + count, put_hs)
            pairs(first, first + count, put_gr)

        pairs(first, first + count, put_e)
        start_own(part)

    outer_part(0)
    outer_part(1)

    @pl.when(n > 0)
    def _():
        put_hs(0)
        put_hs(NC - 1)

    for m, parts in ((1, (0, 1)), (2, (0,)), (3, (0, 1))):
        @pl.when(n == m)
        def _():
            for part in parts:
                hand_on(m, part)

    for copy in halos[4:]:
        copy.wait_recv()
    pl.semaphore_wait(ready, 3)
    start_own(2)

    @pl.loop(0, 2)
    def _(side):
        first_plane(side * 33 - 1, (8, 16, 24, 32))
        first_plane(side * 31, (7, 15, 23, 31, 39))

    @pl.loop(0, 2)
    def _(side):
        second_plane(side * 30, (0, 8, 16, 24))
        second_plane(side * 30 + 1, (0, 8, 16, 24))

    @pl.when(n > 0)
    def _():
        put_rs(-1)
        put_rs(NC)
        put_gr(0)
        put_gr(NC - 1)

    put_e(0)
    put_e(NC - 1)
    start_own(3)

    @pl.when(n == 0)
    def _():
        @pl.loop(0, NB)
        def _(y):
            for f in FIELDS:
                for x in range(0, NB, 8):
                    o_ref[pl.ds(f * NB * NB + x * NB + y, 8, stride=NB), :] = fine[f, y, pl.ds(x, 8), :]

    def widen(k, rows, own_cols, west, east):
        chain[k][:, rows, pl.ds(0, 8), :] = jnp.where(even, west, lane_down(own_cols))
        chain[k][:, rows, pl.ds(16, 8), :] = jnp.where(even, lane_up(own_cols), east)

    def widen_row(k, row, beside):
        widen(k, row, chain[k][:, row, cols, :], lane_up(beside), lane_down(beside))

    def widen_part(k, part):
        first, count = PARTS[part]
        half = count // 2
        beside = edge[k][:, pl.ds(4 * part, half)]
        one, two = (pl.ds(HALO + first + start, half) for start in (0, half))
        widen(k, one, chain[k][:, one, cols, :], lane_up(beside), lane_down(beside))
        widen(k, two, chain[k][:, two, cols, :], beside, beside)

    def level_rows(k, count, *firsts):
        blocks = [(y, start) for y in firsts for start in (4, 12)]
        out = [strip_rows(chain[k - 1], y, count, start, ctop, cbottom) for y, start in blocks]
        for (y, start), part in zip(blocks, out):
            for f in FIELDS:
                here = (f, pl.ds(y + HALO, count), pl.ds(start, 8), slice(None))
                chain[k][here] = chain[k][here] + part[f]

    def result_rows(m, y, count):
        out = strip_rows(chain[m - 1], y, count, 8, ctop, cbottom)
        for f in FIELDS:
            d = out[f] - gr[f, pl.ds(y, count)]
            low = jnp.where(even, d, lane_down(d))
            high = jnp.where(even, lane_up(d), d)
            for i in range(count):
                for half in range(2):
                    plane = 2 * (y + i) + half
                    for x, part in ((0, low), (1, low), (16, high), (17, high)):
                        total = fine[f, plane, pl.ds(x, 8, stride=2), :] + part[i]
                        o_ref[pl.ds(f * NB * NB + x * NB + plane, 8, stride=2 * NB), :] = total

    def finish(m):
        passes = [[pass_copies(k, m, part) for part in range(3)] for k in range(m)]
        if m == 2:
            hand_on(m, 1)
        for k in range(m):
            own_copies(k, m, 3)[0].wait_recv()
            for copy in passes[k][2]:
                copy.start()
        for k in range(m):
            for part in (0, 1):
                for copy in passes[k][part]:
                    copy.wait()
                widen_part(k, part)
            if m - k > 2:
                widen_row(k, HALO - 2, rim[k][:, 2])
                widen_row(k, HALO + NC + 1, rim[k][:, 3])
        if m == 2:
            for part in (0, 1):
                own_copies(1, 3, part)[0].wait_send()
        for k in range(1, m):
            pl.loop(k + 1, NC - 1 - k, step=2)(lambda y: level_rows(k, 2, y))
        pl.loop(m + 1, NC - 1 - m, step=2)(lambda y: result_rows(m, y, 2))
        for k in range(m):
            for copy in passes[k][2]:
                copy.wait()
            for copy in own_copies(k, m, 2) + own_copies(k, m, 3)[1:]:
                copy.wait_recv()
            for i, row in ((0, HALO + NC - 1), (1, HALO)):
                own_cols = late_own[k, :, i]
                chain[k][:, row, cols, :] = own_cols
                beside = late_rim[k, :, i]
                widen(k, row, own_cols, lane_up(beside), lane_down(beside))
            if m - k > 1:
                widen_row(k, below, rim[k][:, 0])
                widen_row(k, above, rim[k][:, 1])
        for k in range(1, m):
            level_rows(k, m + 1, k - m, NC - 1 - k)
        result_rows(m, 0, m + 1)
        result_rows(m, NC - 1 - m, m + 1)

    for m in (1, 2, 3):
        pl.when(n == m)(lambda: finish(m))

    for copy in halos:
        copy.wait_send()
    for k in (0, 1, 2):
        @pl.when(n == k)
        def _():
            for m in range(k + 1, 4):
                for part in range(4):
                    if not (part < 2 and (k, m) in RELAYED):
                        for copy in own_copies(k, m, part):
                            copy.wait_send()

    @pl.when(n == 3)
    def _():
        for part in (0, 1):
            own_copies(0, 2, part)[0].wait_send()


def body(slice_starts):
    fields = slice_starts[0]
    f32 = jnp.float32
    out = pl.pallas_call(
        kernel,
        out_shape=pltpu.VMEM((5 * NB * NB, 128), f32),
        in_specs=[pl.BlockSpec(memory_space=pltpu.HBM)],
        out_specs=pl.BlockSpec(memory_space=pltpu.VMEM),
        scratch_shapes=[
            pltpu.VMEM((5, 36, 48, 128), f32),
            pltpu.VMEM((5, 34, 48, 128), f32),
            pltpu.VMEM((5, NB, NB, 128), f32),
            pltpu.VMEM((5, NC + 2, 8, 128), f32),
            pltpu.VMEM((5, NC, 8, 128), f32),
            pltpu.VMEM((5, NC, 8, 128), f32),
            pltpu.VMEM((5, NC, 8, 128), f32),
            *[pltpu.VMEM((5, NC + 2 * HALO, 24, 128), f32) for _ in range(3)],
            *[pltpu.VMEM((5, 4, 8, 128), f32) for _ in range(3)],
            *[pltpu.VMEM((5, 7, 8, 128), f32) for _ in range(3)],
            *[pltpu.VMEM((5, 7, 8, 128), f32) for _ in range(3)],
            pltpu.VMEM((3, 5, 2, 8, 128), f32),
            pltpu.VMEM((3, 5, 2, 8, 128), f32),
            pltpu.SemaphoreType.DMA,
            pltpu.SemaphoreType.DMA((12,)),
            pltpu.SemaphoreType.DMA((12,)),
            pltpu.SemaphoreType.DMA((3, 11)),
            pltpu.SemaphoreType.DMA((3, 11)),
            pltpu.SemaphoreType.DMA((3, 14)),
            pltpu.SemaphoreType.DMA((3, 14)),
            pltpu.SemaphoreType.REGULAR,
        ],
        compiler_params=pltpu.CompilerParams(
            collective_id=0, has_side_effects=True, vmem_limit_bytes=60 * 1024 * 1024
        ),
    )(fields)
    return out.reshape((1,) + fields.shape)


def solution(mesh):
    return jax.shard_map(
        body,
        mesh=mesh,
        in_specs=(P("cuts", None, "gx", "gy", None),),
        out_specs=P("cuts", None, "gx", "gy", None),
        check_vma=False,
    )
```

```python
import jax
import jax.numpy as jnp
from jax import lax
from jax.experimental import pallas as pl
from jax.experimental.pallas import tpu as pltpu
from jax.sharding import PartitionSpec as P

TIME_STEP = 0.1
VISCOSITY = 0.2
MESH = pl.DeviceIdType.MESH
NB = 32
NC = 16
X0 = 8
FIELDS = range(5)
HALO = 3
RELAYED = {(1, 3): 2, (0, 2): 3}
PARTS = ((1, 8), (9, 6))


def stencil(C, E, W, N, S, A, B, top, bottom, spacing, step):
    g = step / (2.0 * spacing)
    k = VISCOSITY * step / (spacing * spacing)
    centre = 1.0 - 6.0 * k
    zero = jnp.zeros_like(C[0])
    gu, gv, gw = g * C[0], g * C[1], g * C[2]
    ce, cw = k - gu, k + gu
    cn, cs = k - gv, k + gv
    ca = jnp.where(top, zero, k - gw)
    cb = jnp.where(bottom, zero, k + gw)
    out = []
    for q in range(4):
        out.append(
            (centre * C[q] + ce * E[q] + cw * W[q])
            + (cn * N[q] + cs * S[q])
            + (ca * A[q] + cb * B[q])
        )
    rise_p = jnp.where(top, zero, A[4]) - jnp.where(bottom, zero, B[4])
    rise_w = jnp.where(top, zero, A[2]) - jnp.where(bottom, zero, B[2])
    out[0] = out[0] - g * (E[4] - W[4])
    out[1] = out[1] - g * (N[4] - S[4])
    out[2] = out[2] + (step * C[3] - g * rise_p)
    out[3] = out[3] + step * C[2]
    out.append(C[4] - g * ((E[0] - W[0]) + (N[1] - S[1]) + rise_w))
    return out


def lanes():
    return lax.broadcasted_iota(jnp.int32, (8, 128), 1)


def sublanes():
    return lax.broadcasted_iota(jnp.int32, (8, 128), 0)


def lane_up(v, n=1):
    return pltpu.roll(v, 128 - n, v.ndim - 1)


def lane_down(v, n=1):
    return pltpu.roll(v, n, v.ndim - 1)


def fine_tile(src, dst, ys, yd, rs, rd, top, bottom):
    C = [src[f, ys, pl.ds(rs, 8), :] for f in FIELDS]
    E = [src[f, ys, pl.ds(rs + 1, 8), :] for f in FIELDS]
    W = [src[f, ys, pl.ds(rs - 1, 8), :] for f in FIELDS]
    N = [src[f, ys + 1, pl.ds(rs, 8), :] for f in FIELDS]
    S = [src[f, ys - 1, pl.ds(rs, 8), :] for f in FIELDS]
    A = [lane_up(c) for c in C]
    B = [lane_down(c) for c in C]
    out = stencil(C, E, W, N, S, A, B, top, bottom, 1.0, TIME_STEP)
    for f in FIELDS:
        dst[f, yd, pl.ds(rd, 8), :] = out[f]


def restrict_row(src, y, x0, even):
    out = []
    for f in FIELDS:
        halves = []
        for base in (x0, x0 + 16):
            total = None
            for plane in (y, y + 1):
                for start in (base, base + 1):
                    part = src[f, plane, pl.ds(start, 8, stride=2), :]
                    total = part if total is None else total + part
            halves.append(total)
        low, high = halves
        out.append(0.125 * jnp.where(even, low + lane_up(low), high + lane_down(high)))
    return out


def coarse_row(C, N, S, H, even, sub, top, bottom):
    E, W = [], []
    for f in FIELDS:
        r_w = pltpu.roll(C[f], 1, 0)
        r_e = pltpu.roll(C[f], 7, 0)
        mixed = jnp.where(sub == 0, jnp.where(even, r_w, H[f]), jnp.where(even, H[f], r_e))
        swapped = jnp.where(even, lane_up(mixed), lane_down(mixed))
        W.append(jnp.where(sub == 0, swapped, r_w))
        E.append(jnp.where(sub == 7, swapped, r_e))
    A = [lane_up(c, 2) for c in C]
    B = [lane_down(c, 2) for c in C]
    return stencil(C, E, W, N, S, A, B, top, bottom, 2.0, 2.0 * TIME_STEP)


def strip_rows(state, y, count, start, top, bottom):
    rows = pl.ds(y + HALO, count)
    here, east, west = (pl.ds(start + shift, 8) for shift in (0, 1, -1))
    C = [state[f, rows, here, :] for f in FIELDS]
    E = [state[f, rows, east, :] for f in FIELDS]
    W = [state[f, rows, west, :] for f in FIELDS]
    N = [state[f, pl.ds(y + HALO + 1, count), here, :] for f in FIELDS]
    S = [state[f, pl.ds(y + HALO - 1, count), here, :] for f in FIELDS]
    A = [lane_up(c, 2) for c in C]
    B = [lane_down(c, 2) for c in C]
    return stencil(C, E, W, N, S, A, B, top, bottom, 2.0, 2.0 * TIME_STEP)


def kernel(x_ref, o_ref, s0, s1, fine, rs, hs, gr, cout, chain0, chain1, chain2, rim0, rim1, rim2,
           packed0, packed1, packed2, edge0, edge1, edge2, late_own, late_rim, load_sem, halo_send, halo_recv, chain_send, chain_recv, pass_send, pass_recv, ready):
    n = lax.axis_index("cuts")
    gx = lax.axis_index("gx")
    gy = lax.axis_index("gy")
    chain, rim = (chain0, chain1, chain2), (rim0, rim1, rim2)
    packed, edge = (packed0, packed1, packed2), (edge0, edge1, edge2)

    def at(dn, dx, dy):
        return (lax.rem(n + 4 + dn, 4), lax.rem(gx + 8 + dx, 8), lax.rem(gy + 8 + dy, 8))

    def remote(src, dst, where, send_sem, recv_sem):
        return pltpu.make_async_remote_copy(
            src_ref=src, dst_ref=dst, send_sem=send_sem, recv_sem=recv_sem,
            device_id=at(*where), device_id_type=MESH,
        )

    partners = [(0, dx, dy) for dx in (0, 1, -1) for dy in (1, -1, 0) if (dx, dy) != (0, 0)]
    partners += [(dn, 0, 0) for dn in (1, 2, 3)]
    barrier = pltpu.get_barrier_semaphore()
    for p in partners:
        pl.semaphore_signal(barrier, inc=1, device_id=at(*p), device_id_type=MESH)

    @pl.loop(0, NB)
    def _(y):
        pltpu.make_async_copy(
            x_ref.at[:, :, y, :], s0.at[:, y + 2, pl.ds(X0, NB), :], load_sem
        ).start()

    pl.semaphore_wait(barrier, len(partners))
    for dn in (1, 2, 3):
        pl.semaphore_signal(ready, inc=1, device_id=at(dn, 0, 0), device_id_type=MESH)

    halos = []

    def send(src, dst, dx, dy):
        i = len(halos)
        copy = remote(src, dst, (0, dx, dy), halo_send.at[i], halo_recv.at[i])
        copy.start()
        halos.append(copy)

    own, rows = pl.ds(2, NB), pl.ds(X0, NB)
    for step in range(2):
        send(x_ref.at[:, 30 + step, :, :], s0.at[:, own, 6 + step, :], 1, 0)
        send(x_ref.at[:, step, :, :], s0.at[:, own, 40 + step, :], -1, 0)
    for dx, x_from, x_to in ((1, 31, 7), (-1, 0, 40)):
        for dy, y_from, y_to in ((1, 31, 1), (-1, 0, 34)):
            send(x_ref.at[:, x_from, y_from, :], s0.at[:, y_to, x_to, :], dx, dy)

    for step in range(2):
        send(x_ref.at[:, :, 30 + step, :], s0.at[:, step, rows, :], 0, 1)
        send(x_ref.at[:, :, step, :], s0.at[:, 34 + step, rows, :], 0, -1)

    lane, sub = lanes(), sublanes()
    even = lane % 2 == 0
    top, bottom = lane == 127, lane == 0
    ctop, cbottom = lane >= 126, lane <= 1

    def first_plane(y, starts):
        for r in starts:
            fine_tile(s0, s1, y + 2, y + 1, r, r, top, bottom)

    def second_plane(y, starts):
        for r in starts:
            fine_tile(s1, fine, y + 1, y, r + X0, r, top, bottom)

    def put_rs(j):
        out = restrict_row(s0, 2 * j + 2, X0, even)
        for f in FIELDS:
            rs[f, j + 1] = out[f]

    def put_hs(j):
        for f in FIELDS:
            total = None
            for plane in (2 * j + 2, 2 * j + 3):
                west = s0[f, plane, pl.ds(6, 8), :] + s0[f, plane, pl.ds(7, 8), :]
                east = s0[f, plane, pl.ds(33, 8), :] + s0[f, plane, pl.ds(34, 8), :]
                part = jnp.where(sub == 0, west, east)
                total = part if total is None else total + part
            hs[f, j] = 0.125 * (total + jnp.where(even, lane_up(total), lane_down(total)))

    def put_gr(j):
        C = [rs[f, j + 1] for f in FIELDS]
        N = [rs[f, j + 2] for f in FIELDS]
        S = [rs[f, j] for f in FIELDS]
        H = [hs[f, j] for f in FIELDS]
        out = coarse_row(C, N, S, H, even, sub, ctop, cbottom)
        for f in FIELDS:
            gr[f, j] = out[f]

    def put_e(j):
        out = restrict_row(fine, 2 * j, 0, even)
        for f in FIELDS:
            cout[f, lax.rem(j + 1, NC)] = out[f] - gr[f, j]

    def pairs(low, high, *jobs):
        @pl.loop(low, high, step=2)
        def _(j):
            for job in jobs:
                job(j)
                job(j + 1)

    pltpu.make_async_copy(x_ref, s0.at[:, own, rows, :], load_sem).wait()
    pairs(1, NB - 1, lambda y: first_plane(y, (15, 23, 31)))
    pairs(2, NB - 2, lambda y: second_plane(y, (8, 16)))

    @pl.when(n == 0)
    def _():
        gr[...] = jnp.zeros_like(gr)

    @pl.when(n > 0)
    def _():
        pairs(0, NC, put_rs)

    for copy in halos[:4]:
        copy.wait_recv()
    cols = pl.ds(8, 8)
    below, above = HALO - 1, HALO + NC

    def own_copies(k, m, part):
        def copy(src, dst, dy, i):
            return remote(src, dst, (m - k, 0, dy), chain_send.at[m - k - 1, i], chain_recv.at[k, i])

        if part == 3:
            copies = [
                copy(cout.at[:, pl.ds(0, 2)], late_own.at[k], 0, 1),
                copy(cout.at[:, 0], chain[k].at[:, below, cols, :], 1, 2),
                copy(cout.at[:, 1], chain[k].at[:, above, cols, :], -1, 3),
            ]
            few = m - k - 1
            if few:
                for row, dy in ((0, 1), (1, -1)):
                    for span, dx in ((pl.ds(8 - few, few), 1), (pl.ds(0, few), -1)):
                        i = len(copies) + 4
                        copies.append(remote(
                            cout.at[:, row, span, :], rim[k].at[:, row, span, :], (m - k, dx, dy),
                            chain_send.at[m - k - 1, i], chain_recv.at[k, i],
                        ))
            return copies
        if part == 2:
            if (k, m) != (1, 3):
                return []
            return [
                copy(cout.at[:, 15], chain[k].at[:, below - 1, cols, :], 1, 4),
                copy(cout.at[:, 2], chain[k].at[:, above + 1, cols, :], -1, 5),
            ]
        first, count = PARTS[part]
        dst = chain[k].at[:, pl.ds(HALO + first, count), cols, :]
        i = (0, 6)[part]
        if (k, m) in RELAYED:
            dn = m - RELAYED[k, m]
            return [remote(dst, dst, (dn, 0, 0), chain_send.at[m - k - 1, i], chain_recv.at[k, i])]
        return [copy(cout.at[:, pl.ds(first + 1, count)], dst, 0, i)]

    def start_own(part):
        for k in (0, 1, 2):
            if part == 2 and k != 1:
                continue

            @pl.when(n == k)
            def _():
                for m in (3, 2, 1):
                    if m > k and not (part < 2 and (k, m) in RELAYED):
                        for copy in own_copies(k, m, part):
                            copy.start()

    def pass_copies(k, m, part):
        copies = []
        wide = m - k

        def add(src, dst, dx, dy):
            i = len(copies) + 6 * part
            copies.append(remote(src, dst, (0, dx, dy), pass_send.at[k, i], pass_recv.at[k, i]))

        low, high = pl.ds(0, wide), pl.ds(8 - wide, wide)
        if part == 2:
            both = pl.ds(0, 2)
            add(late_own.at[k, :, both, high, :], late_rim.at[k, :, both, high, :], 1, 0)
            add(late_own.at[k, :, both, low, :], late_rim.at[k, :, both, low, :], -1, 0)
            return copies
        span = (pl.ds(0, 4), pl.ds(4, 3))[part]
        add(packed[k].at[:, span, high, :], edge[k].at[:, span, high, :], 1, 0)
        add(packed[k].at[:, span, low, :], edge[k].at[:, span, low, :], -1, 0)
        if wide > 1 and (k, m) != (1, 3):
            deep = wide - 1
            src, dst, dy = ((HALO + 1, above + 1, -1), (above - 1 - deep, below - deep, 1))[part]
            add(chain[k].at[:, pl.ds(src, deep), cols, :], chain[k].at[:, pl.ds(dst, deep), cols, :], 0, dy)
        if wide > 2:
            src, dst, dy = ((HALO + 1, 3, -1), (above - 2, 2, 1))[part]
            add(chain[k].at[:, src, pl.ds(15, 1), :], rim[k].at[:, dst, pl.ds(7, 1), :], 1, dy)
            add(chain[k].at[:, src, pl.ds(8, 1), :], rim[k].at[:, dst, pl.ds(0, 1), :], -1, dy)
        return copies

    def pack(k, part):
        first, count = PARTS[part]
        half = count // 2
        one = chain[k][:, pl.ds(HALO + first, half), cols, :]
        two = chain[k][:, pl.ds(HALO + first + half, half), cols, :]
        upper = jnp.where(even, lane_up(two), one)
        lower = jnp.where(even, one, lane_down(two))
        packed[k][:, pl.ds(4 * part, half)] = jnp.where(sub < 4, lower, upper)

    def hand_on(m, part, sources):
        for k in sources:
            own_copies(k, m, part)[0].wait_recv()
            for (first, last), via in RELAYED.items():
                if (first, via) == (k, m):
                    own_copies(first, last, part)[0].start()
            pack(k, part)
            for copy in pass_copies(k, m, part):
                copy.start()

    def outer_part(part):
        first, count = PARTS[part]
        pairs((1, 19)[part], (19, 31)[part], lambda y: first_plane(y, (7, 39)))
        pairs(2 * first, 2 * (first + count), lambda y: second_plane(y, (0, 24)))

        @pl.when(n > 0)
        def _():
            pairs(first, first + count, put_hs)
            pairs(first, first + count, put_gr)

        pairs(first, first + count, put_e)
        start_own(part)

    outer_part(0)
    outer_part(1)

    @pl.when(n > 0)
    def _():
        put_hs(0)
        put_hs(NC - 1)

    arrivals = (
        (1, ((0, (0,)), (1, (0,)))),
        (2, ((0, (1,)), (1, (1,)), (0, (0,)))),
        (3, ((0, (0, 2)), (1, (0,)), (0, (1,)), (1, (2, 1)))),
    )
    for m, order in arrivals:
        @pl.when(n == m)
        def _():
            for part, sources in order:
                hand_on(m, part, sources)

    for copy in halos[4:]:
        copy.wait_recv()
    pl.semaphore_wait(ready, 3)
    start_own(2)

    for y in (-1, NB):
        first_plane(y, (8, 16, 24, 32))
    for y in (0, NB - 1):
        first_plane(y, (7, 15, 23, 31, 39))
    for y in (0, 1, NB - 2, NB - 1):
        second_plane(y, (0, 8, 16, 24))

    @pl.when(n > 0)
    def _():
        put_rs(-1)
        put_rs(NC)
        put_gr(0)
        put_gr(NC - 1)

    put_e(0)
    put_e(NC - 1)
    start_own(3)

    @pl.when(n == 0)
    def _():
        @pl.loop(0, NB)
        def _(y):
            for f in FIELDS:
                for x in range(0, NB, 8):
                    o_ref[pl.ds(f * NB * NB + x * NB + y, 8, stride=NB), :] = fine[f, y, pl.ds(x, 8), :]

    def widen(k, rows, own_cols, west, east):
        chain[k][:, rows, pl.ds(0, 8), :] = jnp.where(even, west, lane_down(own_cols))
        chain[k][:, rows, pl.ds(16, 8), :] = jnp.where(even, lane_up(own_cols), east)

    def widen_row(k, row, beside):
        widen(k, row, chain[k][:, row, cols, :], lane_up(beside), lane_down(beside))

    def widen_part(k, part):
        first, count = PARTS[part]
        half = count // 2
        beside = edge[k][:, pl.ds(4 * part, half)]
        one, two = (pl.ds(HALO + first + start, half) for start in (0, half))
        widen(k, one, chain[k][:, one, cols, :], lane_up(beside), lane_down(beside))
        widen(k, two, chain[k][:, two, cols, :], beside, beside)

    def level_rows(k, count, *firsts):
        blocks = [(y, start) for y in firsts for start in (4, 12)]
        out = [strip_rows(chain[k - 1], y, count, start, ctop, cbottom) for y, start in blocks]
        for (y, start), part in zip(blocks, out):
            for f in FIELDS:
                here = (f, pl.ds(y + HALO, count), pl.ds(start, 8), slice(None))
                chain[k][here] = chain[k][here] + part[f]

    def result_rows(m, count, *firsts):
        out = [strip_rows(chain[m - 1], y, count, 8, ctop, cbottom) for y in firsts]
        for (y, terms), f in [(block, f) for block in zip(firsts, out) for f in FIELDS]:
            d = terms[f] - gr[f, pl.ds(y, count)]
            low = jnp.where(even, d, lane_down(d))
            high = jnp.where(even, lane_up(d), d)
            for i in range(count):
                for half in range(2):
                    plane = 2 * (y + i) + half
                    for x, part in ((0, low), (1, low), (16, high), (17, high)):
                        total = fine[f, plane, pl.ds(x, 8, stride=2), :] + part[i]
                        o_ref[pl.ds(f * NB * NB + x * NB + plane, 8, stride=2 * NB), :] = total

    def finish(m):
        passes = [[pass_copies(k, m, part) for part in range(3)] for k in range(m)]
        if m == 2:
            hand_on(m, 1, (0,))
        for k in range(m):
            own_copies(k, m, 3)[0].wait_recv()
            for copy in passes[k][2]:
                copy.start()
        for k in range(m):
            for part in (0, 1):
                for copy in passes[k][part]:
                    copy.wait()
                widen_part(k, part)
            if m - k > 2:
                widen_row(k, HALO - 2, rim[k][:, 2])
                widen_row(k, HALO + NC + 1, rim[k][:, 3])
        if m == 2:
            for part in (0, 1):
                own_copies(1, 3, part)[0].wait_send()
        for k in range(1, m):
            pl.loop(k + 1, NC - 1 - k, step=2)(lambda y: level_rows(k, 2, y))
        pl.loop(m + 1, NC - 1 - m, step=2)(lambda y: result_rows(m, 2, y))
        for k in range(m):
            for copy in passes[k][2]:
                copy.wait()
            for copy in own_copies(k, m, 2) + own_copies(k, m, 3)[1:]:
                copy.wait_recv()
            for i, row in ((0, HALO + NC - 1), (1, HALO)):
                own_cols = late_own[k, :, i]
                chain[k][:, row, cols, :] = own_cols
                beside = late_rim[k, :, i]
                widen(k, row, own_cols, lane_up(beside), lane_down(beside))
            if m - k > 1:
                widen_row(k, below, rim[k][:, 0])
                widen_row(k, above, rim[k][:, 1])
        for k in range(1, m):
            level_rows(k, m + 1, k - m, NC - 1 - k)
        result_rows(m, m + 1, 0, NC - 1 - m)

    for m in (1, 2, 3):
        pl.when(n == m)(lambda: finish(m))

    for copy in halos:
        copy.wait_send()
    for k in (0, 1, 2):
        @pl.when(n == k)
        def _():
            for m in range(k + 1, 4):
                for part in range(4):
                    if not (part < 2 and (k, m) in RELAYED):
                        for copy in own_copies(k, m, part):
                            copy.wait_send()

    @pl.when(n == 3)
    def _():
        for part in (0, 1):
            own_copies(0, 2, part)[0].wait_send()


def body(slice_starts):
    fields = slice_starts[0]
    f32 = jnp.float32
    out = pl.pallas_call(
        kernel,
        out_shape=pltpu.VMEM((5 * NB * NB, 128), f32),
        in_specs=[pl.BlockSpec(memory_space=pltpu.HBM)],
        out_specs=pl.BlockSpec(memory_space=pltpu.VMEM),
        scratch_shapes=[
            pltpu.VMEM((5, 36, 48, 128), f32),
            pltpu.VMEM((5, 34, 48, 128), f32),
            pltpu.VMEM((5, NB, NB, 128), f32),
            pltpu.VMEM((5, NC + 2, 8, 128), f32),
            pltpu.VMEM((5, NC, 8, 128), f32),
            pltpu.VMEM((5, NC, 8, 128), f32),
            pltpu.VMEM((5, NC, 8, 128), f32),
            *[pltpu.VMEM((5, NC + 2 * HALO, 24, 128), f32) for _ in range(3)],
            *[pltpu.VMEM((5, 4, 8, 128), f32) for _ in range(3)],
            *[pltpu.VMEM((5, 7, 8, 128), f32) for _ in range(3)],
            *[pltpu.VMEM((5, 7, 8, 128), f32) for _ in range(3)],
            pltpu.VMEM((3, 5, 2, 8, 128), f32),
            pltpu.VMEM((3, 5, 2, 8, 128), f32),
            pltpu.SemaphoreType.DMA,
            pltpu.SemaphoreType.DMA((12,)),
            pltpu.SemaphoreType.DMA((12,)),
            pltpu.SemaphoreType.DMA((3, 11)),
            pltpu.SemaphoreType.DMA((3, 11)),
            pltpu.SemaphoreType.DMA((3, 14)),
            pltpu.SemaphoreType.DMA((3, 14)),
            pltpu.SemaphoreType.REGULAR,
        ],
        compiler_params=pltpu.CompilerParams(
            collective_id=0, has_side_effects=True, vmem_limit_bytes=60 * 1024 * 1024
        ),
    )(fields)
    return out.reshape((1,) + fields.shape)


def solution(mesh):
    return jax.shard_map(
        body,
        mesh=mesh,
        in_specs=(P("cuts", None, "gx", "gy", None),),
        out_specs=P("cuts", None, "gx", "gy", None),
        check_vma=False,
    )
```
